256 devices in a mesh: rep: 16 (over y, z_hi, core), fsdp: 16 (over x, z_lo).
Axes of the slice: x: 4, y: 4, z: 8 (z_hi: 2, z_lo: 4; z = z_hi * 4 + z_lo), core: 2. Of those that a mesh axis runs over, the one named last changes fastest.
Arguments:
- tokens: bfloat16 [98304, 4096], P(('rep', 'fsdp')), may hold values from -24 to 24
- cotangent: bfloat16 [98304, 1024], P(('rep', 'fsdp')), may hold values from -6 to 6
- weight: bfloat16 [4096, 1024], P('fsdp'), may hold values from -0.1875 to 0.1875
- moment: float32 [4096, 640], P('fsdp'), may hold values from -6 to 6
- second: float32 [4096, 640], P('fsdp'), may hold values from 0.25 to 4
- delayed: float32 [16, 4096, 384], P('rep', 'fsdp'), may hold values from -0.12 to 0.12
Outputs:
- grad_input: bfloat16 [98304, 4096], P(('rep', 'fsdp'))
- moment_next: float32 [4096, 640], P('fsdp')
- second_next: float32 [4096, 640], P('fsdp')
- adam_step: float32 [4096, 640], P('fsdp')
- host_grad: float32 [4096, 384], P('fsdp')
The draws below stay inside these ranges and needn't reach their ends.
All inputs are finite; a program needn't handle non-finite values.
Results may differ from the reference program's by a relative error of at most 0.0038.
Values may be sent and summed in bfloat16 or wider, within the bound.
No kernel may reach another device: no remote copies, remote signals or barrier semaphores. Data moves between devices by JAX's collectives and lax.ppermute only.
A program may use at most 128 MiB of HBM per device.

```python
import math
import jax
import jax.numpy as jnp

D = 4096
KV = 1024
DEVC = 640
HOSTC = 384
GROUPS = 16
TOKENS = 98304


def spiked(array, key, source, target, shards_of, factor):
    owner, partner = [(jnp.arange(array.shape[position]) // (array.shape[position] // shards_of)).reshape([-1 if axis == position else 1 for axis in range(array.ndim)]) for position in (source, target)]
    chosen = jax.random.permutation(key, shards_of)[partner]
    strong = (owner == chosen) | (owner == (partner + shards_of // 2) % shards_of)
    return jnp.where(strong, factor * array, array)


def block_levels(stream_key, dims, shards, least, high):
    level = 1.0
    for position, shards_of in shards:
        draws = jax.random.uniform(jax.random.fold_in(jax.random.fold_in(stream_key, 6), position), (shards_of,), jnp.float32, least / len(shards), high / len(shards))
        level = level * jnp.repeat(jnp.exp(draws), dims[position] // shards_of).reshape((-1,) + (1,) * (len(dims) - 1 - position))
    return level


def bell_draw(key, shape, scale, reach, split=(), held_as=jnp.bfloat16):
    gain = block_levels(key, shape, split, -0.22, 0.18) if split else 1.0
    result = jax.random.normal(key, shape, jnp.float32) * scale * gain
    return jnp.minimum(jnp.maximum(result, -reach), reach).astype(held_as)


def heavy_noise(own_key, shape, width, bound, cuts, heavy, dtype=jnp.bfloat16):
    array = width * jax.random.normal(own_key, shape, jnp.float32)
    if cuts:
        array = array * block_levels(own_key, shape, cuts, -0.22, 0.18)
    return jnp.clip(spiked(array, jax.random.fold_in(own_key, 3), *heavy), -bound, bound).astype(dtype)


def setup_inputs(seed: int = 0) -> dict:
    arg_keys = jax.random.split(jax.random.key(seed), 7)
    tokens = heavy_noise(arg_keys[0], (TOKENS, D), 1.0, 24.0, ((0, 256),), (0, 1, 256, 6.0))
    cotangent = bell_draw(arg_keys[1], (TOKENS, KV), 1.0, 6.0, ((0, 256),))
    weight = bell_draw(arg_keys[2], (D, KV), KV ** -0.5, 0.1875, ((0, 16),))
    moment = bell_draw(arg_keys[3], (D, DEVC), 1.0, 6.0, ((0, 16),), jnp.float32)
    second = jnp.clip(jnp.exp(math.log(4.0) - 2.7725887 * jax.random.uniform(arg_keys[4], (D, DEVC), jnp.float32) ** block_levels(arg_keys[4], (D, DEVC), ((0, 16),), -0.2, 0.2)), 0.25, 4.0)
    delayed = bell_draw(arg_keys[5], (GROUPS, D, HOSTC), 0.02, 0.12, ((0, 16), (1, 16)), jnp.float32)
    return dict(tokens=tokens, cotangent=cotangent, weight=weight, moment=moment, second=second, delayed=delayed)


def reference(tokens, cotangent, weight, moment, second, delayed):
    refreshed = (weight[:, DEVC:].astype(jnp.float32) + delayed[0]).astype(jnp.bfloat16)
    current = jnp.concatenate([weight[:, :DEVC], refreshed], axis=1)
    grad_input = jnp.dot(cotangent, current.T, preferred_element_type=jnp.float32).astype(jnp.bfloat16)
    grad = jnp.dot(tokens.T, cotangent, preferred_element_type=jnp.float32) * TOKENS ** (-0.5)
    device_grad = grad[:, :DEVC]
    moment_next = 0.9 * moment + 0.1 * device_grad
    second_next = 0.95 * second + 0.05 * device_grad * device_grad
    adam_step = moment_next / (1.0 - 0.9 ** 20) / (jnp.sqrt(second_next / (1.0 - 0.95 ** 20)) + 1e-08)
    return (grad_input, moment_next, second_next, adam_step, grad[:, DEVC:])
```

```python
import jax
import jax.numpy as jnp
from jax import lax
from jax.experimental import pallas as pl
from jax.experimental.pallas import tpu as pltpu
from jax.sharding import PartitionSpec as P

AXES = ("rep", "fsdp")
SIZES = {"y": 4, "zh": 2, "c": 2, "x": 4, "zl": 4}
F32 = jnp.float32
BF16 = jnp.bfloat16


def unflatten(i):
    c = {}
    for name in ("zl", "x", "c", "zh", "y"):
        c[name] = i % SIZES[name]
        i //= SIZES[name]
    return c


def flatten(c):
    i = 0
    for name in ("y", "zh", "c", "x", "zl"):
        i = i * SIZES[name] + c[name]
    return i


def send(value, route):
    pairs = []
    for i in range(256):
        target = route(unflatten(i))
        if target is not None:
            pairs.append((i, flatten(target)))
    return lax.ppermute(value, AXES, pairs)


def partner(axis, first):
    def route(c):
        mask = 1 if (c["c"] == 0) == first else 3
        t = dict(c)
        t[axis] = c[axis] ^ mask
        if axis == "zl" and mask == 3 and c["zl"] in (0, 3):
            t["zh"] = 1 - c["zh"]
        return t

    return route


def flip(axis):
    def route(c):
        t = dict(c)
        t[axis] = 1 - c[axis]
        return t

    return route


def where_am_i():
    rep, fsdp = lax.axis_index("rep"), lax.axis_index("fsdp")
    return {"y": rep // 4, "zh": rep // 2 % 2, "c": rep % 2, "x": fsdp // 4, "zl": fsdp % 4}


def pick(value, index, dim):
    return lax.dynamic_index_in_dim(value, index, dim, keepdims=False)


def halve(value, dim, axis, me, wire):
    p = me[axis]
    a = jnp.where(me["c"] == 0, 1, 3)
    b = 4 - a
    got = send(
        jnp.stack([pick(value, p ^ a, dim), pick(value, p ^ 2, dim)]).astype(wire), partner(axis, True)
    )
    far = pick(value, p ^ b, dim) + got[1].astype(F32)
    near = pick(value, p, dim) + got[0].astype(F32)
    return near + send(far.astype(wire), partner(axis, False)).astype(F32)


def double(value, axis):
    pair = jnp.stack([value, send(value, partner(axis, False))])
    return jnp.concatenate([pair, send(pair, partner(axis, True))])


def places(p, core):
    b = jnp.where(core == 0, 3, 1)
    out = []
    for j in range(4):
        r = p ^ j
        out.append(jnp.where(r == 0, 0, jnp.where(r == b, 1, jnp.where(r == 2, 3, 2))))
    return out


def half_kernel(s_ref, t_ref, o_ref):
    other = 1 - s_ref[0]
    for j in range(16):
        start = pl.multiple_of(j * 256 + other * 128, 128)
        o_ref[:, j * 128 : (j + 1) * 128] = t_ref[:, pl.ds(start, 128)]


def mates_half(core, tokens):
    return pl.pallas_call(
        half_kernel,
        out_shape=jax.ShapeDtypeStruct((384, 2048), BF16),
        grid_spec=pltpu.PrefetchScalarGridSpec(
            num_scalar_prefetch=1,
            grid=(4,),
            in_specs=[pl.BlockSpec((96, 4096), lambda i, s: (i, 0))],
            out_specs=pl.BlockSpec((96, 2048), lambda i, s: (i, 0)),
        ),
        cost_estimate=pl.CostEstimate(flops=0, bytes_accessed=6 << 20, transcendentals=0),
    )(core, tokens)


def grad_kernel(s_ref, t_ref, u_ref, c_ref, d_ref, one_ref, two_ref):
    over_tokens = (((0,), (0,)), ((), ()))
    total = lax.dot_general(t_ref[...], c_ref[...], over_tokens, preferred_element_type=F32)
    total += lax.dot_general(u_ref[...], d_ref[...], over_tokens, preferred_element_type=F32)
    for y in range(4):
        one_ref[y, 0] = total[:, y * 256 : y * 256 + 128]
        two_ref[y, 0] = total[:, y * 256 + 128 : y * 256 + 256]


def chip_gradient(core, tokens, their_tokens, cot, their_cot):
    part = jax.ShapeDtypeStruct((4, 16, 128, 128), F32)
    whole = pl.BlockSpec((384, 1024), lambda j, s: (0, 0))
    return pl.pallas_call(
        grad_kernel,
        out_shape=(part, part),
        grid_spec=pltpu.PrefetchScalarGridSpec(
            num_scalar_prefetch=1,
            grid=(16,),
            in_specs=[
                pl.BlockSpec((384, 128), lambda j, s: (0, 2 * j + s[0])),
                pl.BlockSpec((384, 128), lambda j, s: (0, j)),
                whole,
                whole,
            ],
            out_specs=[pl.BlockSpec((4, 1, 128, 128), lambda j, s: (0, j, 0, 0))] * 2,
        ),
        compiler_params=pltpu.CompilerParams(vmem_limit_bytes=32 << 20),
        cost_estimate=pl.CostEstimate(
            flops=2 * 768 * 2048 * 1024, bytes_accessed=14 << 20, transcendentals=0
        ),
    )(core, tokens, their_tokens, cot, their_cot)


def product(s_ref, cot_ref, w_ref, r_ref, zl):
    at = s_ref[5 + zl]
    rows = jnp.concatenate([w_ref[s_ref[9 + y], at, 0] for y in range(4)])
    host = jnp.concatenate([r_ref[at, s_ref[9 + y], 0] for y in range(4)])
    last = (((1,), (1,)), ((), ()))
    split = rows.shape[1]
    total = lax.dot_general(cot_ref[:, :split], rows, last, preferred_element_type=F32)
    total += lax.dot_general(cot_ref[:, split:], host, last, preferred_element_type=F32)
    return total.astype(BF16)


def theirs_kernel(s_ref, cot_ref, w_ref, r_ref, o_ref):
    for zl in range(4):
        o_ref[:, zl * 128 : zl * 128 + 128] = product(s_ref, cot_ref, w_ref, r_ref, zl)


def ours_kernel(s_ref, cot_ref, w_ref, r_ref, got_ref, o_ref):
    core = s_ref[0]
    for zl in range(4):
        mine = pl.multiple_of(zl * 256 + core * 128, 128)
        other = pl.multiple_of(zl * 256 + 128 - core * 128, 128)
        o_ref[:, pl.ds(mine, 128)] = product(s_ref, cot_ref, w_ref, r_ref, zl)
        o_ref[:, pl.ds(other, 128)] = got_ref[:, zl * 128 : zl * 128 + 128]


def input_gradient(kernel, where, cot, kept, host, got=None):
    width = 512 if got is None else 1024
    more = [] if got is None else [pl.BlockSpec((384, 512), lambda x, s: (0, x))]
    return pl.pallas_call(
        kernel,
        out_shape=jax.ShapeDtypeStruct((384, 4 * width), BF16),
        grid_spec=pltpu.PrefetchScalarGridSpec(
            num_scalar_prefetch=1,
            grid=(4,),
            in_specs=[
                pl.BlockSpec((384, 1024), lambda x, s: (0, 0)),
                pl.BlockSpec((4, 4, 1, 32, kept.shape[-1]), lambda x, s: (0, 0, s[1 + x], 0, 0)),
                pl.BlockSpec((4, 4, 1, 32, host.shape[-1]), lambda x, s: (0, 0, s[1 + x], 0, 0)),
            ]
            + more,
            out_specs=pl.BlockSpec((384, width), lambda x, s: (0, x)),
        ),
        compiler_params=pltpu.CompilerParams(vmem_limit_bytes=32 << 20),
        cost_estimate=pl.CostEstimate(
            flops=2 * 384 * 2048 * 1024, bytes_accessed=7 << 20, transcendentals=0
        ),
    )(*([where, cot, kept, host] + ([] if got is None else [got])))


def scatter_from_root(refreshed, me):
    pieces = refreshed.reshape(2, 4, 32, refreshed.shape[1])

    def over_y(y):
        return lambda c: dict(c, y=y) if (c["y"], c["zh"], c["c"]) == (0, 0, 0) else None

    def over_rest(zh, core):
        return lambda c: dict(c, zh=zh, c=core) if (c["zh"], c["c"]) == (0, 0) else None

    got = [pieces[:, 0]] + [send(pieces[:, y], over_y(y)) for y in (1, 2, 3)]
    y = me["y"]
    both = jnp.where(y == 0, got[0], jnp.where(y == 1, got[1], jnp.where(y == 2, got[2], got[3])))
    rest = {(0, 0): both[0]}
    for zh, core in ((1, 1), (1, 0), (0, 1)):
        rest[zh, core] = send(both[core], over_rest(zh, core))
    zero = jnp.where(me["c"] == 0, rest[0, 0], rest[0, 1])
    one = jnp.where(me["c"] == 0, rest[1, 0], rest[1, 1])
    return jnp.where(me["zh"] == 0, zero, one)


def on_device(tokens, cotangent, weight, moment, second, delayed):
    me = where_am_i()
    device_cols = moment.shape[1]
    norm_factor = (tokens.shape[0] * lax.axis_size("rep") * lax.axis_size("fsdp")) ** (-0.5)
    core = me["c"].astype(jnp.int32).reshape(1)

    their_cot = send(cotangent, flip("c"))
    their_tokens = send(mates_half(core, tokens), flip("c"))

    refreshed = (weight[:, device_cols:].astype(F32) + delayed[0]).astype(BF16)
    kept = lax.dynamic_slice(weight, (me["c"] * 128 + me["y"] * 32, 0), (32, device_cols))
    kept = double(double(double(kept, "x"), "zl"), "y")
    host = scatter_from_root(refreshed, me)
    host = double(double(double(host, "x"), "y"), "zl")

    one, two = chip_gradient(core, tokens, their_tokens, cotangent, their_cot)
    one = one.reshape(4, 4, 4, 128, 128)
    two = two.reshape(4, 4, 4, 128, 128)
    one = halve(one, 1, "x", me, BF16)
    two = halve(two, 2, "zl", me, BF16)
    one = halve(one, 0, "y", me, BF16)
    two = halve(two, 1, "x", me, BF16)
    one = halve(one, 0, "zl", me, F32)
    two = halve(two, 0, "y", me, F32)
    total = jnp.stack([one, two]).astype(BF16)
    total = total.astype(F32) + send(total, flip("zh")).astype(F32)
    mine = double(total, "y")
    other = send(mine, flip("c"))

    def in_place(blocks, of_core):
        at = places(me["y"], of_core)
        return jnp.concatenate([pick(blocks, at[y], 0)[h] for y in range(4) for h in range(2)], axis=1)

    is_first = me["c"] == 0
    mine, other = in_place(mine, me["c"]), in_place(other, 1 - me["c"])
    grad = norm_factor * jnp.concatenate(
        [jnp.where(is_first, mine, other), jnp.where(is_first, other, mine)]
    )
    device_grad = grad[:, :device_cols]
    moment_next = 0.9 * moment + 0.1 * device_grad
    second_next = 0.95 * second + 0.05 * device_grad * device_grad
    adam_step = moment_next / (1.0 - 0.9**20) / (jnp.sqrt(second_next / (1.0 - 0.95**20)) + 1e-08)

    where = jnp.stack(
        [me["c"]] + [at for axis in ("x", "zl", "y") for at in places(me[axis], me["c"])]
    ).astype(jnp.int32)
    got = send(input_gradient(theirs_kernel, where, their_cot, kept, host), flip("c"))
    grad_input = input_gradient(ours_kernel, where, cotangent, kept, host, got)
    return (grad_input, moment_next, second_next, adam_step, grad[:, device_cols:])


def solution(mesh):
    placed = (
        P(("rep", "fsdp"), None),
        P(("rep", "fsdp"), None),
        P("fsdp", None),
        P("fsdp", None),
        P("fsdp", None),
        P("rep", "fsdp", None),
    )
    return jax.shard_map(
        on_device,
        mesh=mesh,
        in_specs=placed,
        out_specs=(
            P(("rep", "fsdp"), None),
            P("fsdp", None),
            P("fsdp", None),
            P("fsdp", None),
            P("fsdp", None),
        ),
        check_vma=False,
    )
```

```python
import functools

import jax
import jax.numpy as jnp
from jax import lax
from jax.experimental import pallas as pl
from jax.experimental.pallas import tpu as pltpu
from jax.sharding import PartitionSpec as P

AXES = ("rep", "fsdp")
SIZES = {"y": 4, "zh": 2, "c": 2, "x": 4, "zl": 4}
HOST_PLACES = (
    (0, 1, 2, 3),
    (1, 0, 2, 3),
    (3, 2, 0, 1),
    (3, 2, 1, 0),
    (1, 0, 3, 2),
    (0, 1, 3, 2),
    (2, 3, 1, 0),
    (2, 3, 0, 1),
)
F32 = jnp.float32
BF16 = jnp.bfloat16


def unflatten(i):
    c = {}
    for name in ("zl", "x", "c", "zh", "y"):
        c[name] = i % SIZES[name]
        i //= SIZES[name]
    c["c"] ^= c["x"] + c["y"] + c["zl"] & 1
    return c


def flatten(c):
    c = dict(c, c=c["c"] ^ (c["x"] + c["y"] + c["zl"] & 1))
    i = 0
    for name in ("y", "zh", "c", "x", "zl"):
        i = i * SIZES[name] + c[name]
    return i


def send(value, route):
    pairs = []
    for i in range(256):
        target = route(unflatten(i))
        if target is not None:
            pairs.append((i, flatten(target)))
    return lax.ppermute(value, AXES, pairs)


def neighbour(axis, mask):
    def route(c):
        t = dict(c)
        t[axis] = c[axis] ^ mask
        if axis == "zl" and mask == 3 and c["zl"] in (0, 3):
            t["zh"] = 1 - c["zh"]
        return t

    return route


def partner(axis, first):
    def route(c):
        return neighbour(axis, 1 if (c["c"] == 0) == first else 3)(c)

    return route


def flip(axis):
    def route(c):
        t = dict(c)
        t[axis] = 1 - c[axis]
        return t

    return route


def where_am_i():
    rep, fsdp = lax.axis_index("rep"), lax.axis_index("fsdp")
    y, x, zl = rep // 4, fsdp // 4, fsdp % 4
    return {"y": y, "zh": rep // 2 % 2, "c": rep % 2 ^ (x + y + zl) % 2, "x": x, "zl": zl}


def ride(value, rider, route):
    rows = value.size // 128
    got = send(jnp.concatenate([value.reshape(rows, 128), rider]), route)
    return got[:rows].reshape(value.shape), got[rows:]


def together(*values):
    return lax.optimization_barrier(values)


def places(p, core):
    b = jnp.where(core == 0, 3, 1)
    out = []
    for j in range(4):
        r = p ^ j
        out.append(jnp.where(r == 0, 0, jnp.where(r == b, 1, jnp.where(r == 2, 3, 2))))
    return out


def orders(p, core):
    a = jnp.where(core == 0, 1, 3)
    return [p ^ 2, p ^ a, p ^ a ^ 2, p]


def chosen(s_ref, t_ref):
    cuts = [pl.multiple_of(s_ref[5 + k] * 256 + s_ref[0] * 128, 128) for k in range(4)]
    return jnp.concatenate([t_ref[:, pl.ds(cut, 128)] for cut in cuts], axis=1)


def columns(s_ref, c_ref, half, places):
    cuts = [pl.multiple_of(s_ref[9 + y] * 256 + half * 128, 128) for y in places]
    return jnp.concatenate([c_ref[:, pl.ds(cut, 128)] for cut in cuts], axis=1).T


def grad_kernel(keep, s_ref, t_hbm, u_hbm, c_hbm, d_hbm, one_ref, two_ref, t, u, c, d, sems):
    places = (2, 3) if keep else (0, 1)
    loads = [pltpu.make_async_copy(c_hbm, c, sems.at[0]), pltpu.make_async_copy(d_hbm, d, sems.at[1])]
    for i in range(4):
        cut = pl.ds(pl.multiple_of(s_ref[1 + i] * 1024, 1024), 1024)
        loads.append(pltpu.make_async_copy(t_hbm.at[:, cut], t.at[i], sems.at[2 + 2 * i]))
        loads.append(pltpu.make_async_copy(u_hbm.at[:, cut], u.at[i], sems.at[3 + 2 * i]))
    for load in loads:
        load.start()
    for load in loads[:2]:
        load.wait()
    one_cot = jnp.concatenate([columns(s_ref, r, 0, range(4)) for r in (c, d)], axis=1)
    two_cot = jnp.concatenate([columns(s_ref, r, 1, places) for r in (c, d)], axis=1)
    for i in range(4):
        for load in loads[2 + 2 * i : 4 + 2 * i]:
            load.wait()
        rows = jnp.concatenate([chosen(s_ref, r) for r in (t.at[i], u.at[i])], axis=0)
        if i in places:
            total = jnp.dot(one_cot, rows, preferred_element_type=F32).astype(one_ref.dtype)
            for y in range(4):
                for k in range(4):
                    one_ref[i - places[0], y, k] = total[y * 128 : y * 128 + 128, k * 128 : k * 128 + 128]
        total = jnp.dot(two_cot, rows, preferred_element_type=F32).astype(two_ref.dtype)
        for y in range(2):
            for k in range(4):
                two_ref[y, i, k] = total[y * 128 : y * 128 + 128, k * 128 : k * 128 + 128]


def chip_gradient(keep, order, tokens, their_tokens, cot, their_cot):
    dtype = F32 if keep else BF16
    vmem = pl.BlockSpec(memory_space=pltpu.VMEM)
    return pl.pallas_call(
        functools.partial(grad_kernel, keep),
        out_shape=(jax.ShapeDtypeStruct((2, 4, 4, 128, 128), dtype),) * 2,
        in_specs=[pl.BlockSpec(memory_space=pltpu.SMEM)] + [pl.BlockSpec(memory_space=pl.ANY)] * 4,
        out_specs=[vmem] * 2,
        scratch_shapes=[pltpu.VMEM((4, 384, 1024), BF16)] * 2
        + [pltpu.VMEM((384, 1024), BF16)] * 2
        + [pltpu.SemaphoreType.DMA((10,))],
        compiler_params=pltpu.CompilerParams(vmem_limit_bytes=56 << 20),
        cost_estimate=pl.CostEstimate(
            flops=768 * 2048 * 1024, bytes_accessed=9 << 20, transcendentals=0
        ),
    )(order, tokens, their_tokens, cot, their_cot)


def rows_kernel(s_ref, w_ref, d_ref, kept_ref, host_ref):
    mine = pl.ds(pl.multiple_of(s_ref[0] * 128, 128), 128)
    kept_ref[...] = w_ref[mine, :640].T
    host_ref[...] = (w_ref[:, 640:].astype(F32) + d_ref[0]).astype(BF16).T


def projection_rows(order, weight, delayed):
    vmem = pl.BlockSpec(memory_space=pltpu.VMEM)
    return pl.pallas_call(
        rows_kernel,
        out_shape=(jax.ShapeDtypeStruct((640, 128), BF16), jax.ShapeDtypeStruct((384, 256), BF16)),
        in_specs=[pl.BlockSpec(memory_space=pltpu.SMEM), vmem, vmem],
        out_specs=(vmem, vmem),
        compiler_params=pltpu.CompilerParams(vmem_limit_bytes=16 << 20),
        cost_estimate=pl.CostEstimate(flops=1 << 17, bytes_accessed=1 << 20, transcendentals=0),
    )(order, weight, delayed)


def product(s_ref, cot_ref, w_ref, r_ref, at):
    width = w_ref.shape[-2]
    kept = jnp.concatenate([w_ref[s_ref[5 + zl], at] for zl in range(4)], axis=1)
    host = jnp.concatenate([r_ref[at, s_ref[9 + zl]] for zl in range(4)], axis=1)
    total = jnp.dot(cot_ref[:, :width], kept, preferred_element_type=F32)
    total += jnp.dot(cot_ref[:, width:], host, preferred_element_type=F32)
    return total.astype(BF16)


def theirs_kernel(s_ref, cot_ref, w_ref, r_ref, o_ref):
    for x in range(4):
        at = s_ref[1 + x]
        o_ref[:, x * 512 : x * 512 + 512] = product(s_ref, cot_ref, w_ref, r_ref, at)


def ours_kernel(s_ref, cot_ref, w_ref, r_ref, got_ref, o_ref):
    core = s_ref[0]
    total = product(s_ref, cot_ref, w_ref, r_ref, s_ref[1 + pl.program_id(0)])
    for zl in range(4):
        mine = pl.multiple_of(zl * 256 + core * 128, 128)
        other = pl.multiple_of(zl * 256 + 128 - core * 128, 128)
        o_ref[:, pl.ds(mine, 128)] = total[:, zl * 128 : zl * 128 + 128]
        o_ref[:, pl.ds(other, 128)] = got_ref[:, zl * 128 : zl * 128 + 128]


def their_input_gradient(where, cot, kept, host):
    vmem = pl.BlockSpec(memory_space=pltpu.VMEM)
    return pl.pallas_call(
        theirs_kernel,
        out_shape=jax.ShapeDtypeStruct((384, 2048), BF16),
        in_specs=[pl.BlockSpec(memory_space=pltpu.SMEM), vmem, vmem, vmem],
        out_specs=vmem,
        compiler_params=pltpu.CompilerParams(vmem_limit_bytes=32 << 20),
        cost_estimate=pl.CostEstimate(
            flops=2 * 384 * 2048 * 1024, bytes_accessed=3 << 20, transcendentals=0
        ),
    )(where, cot, kept, host)


def our_input_gradient(where, cot, kept, host, got):
    vmem = pl.BlockSpec(memory_space=pltpu.VMEM)
    return pl.pallas_call(
        ours_kernel,
        out_shape=jax.ShapeDtypeStruct((384, 4096), BF16),
        grid=(4,),
        in_specs=[
            pl.BlockSpec(memory_space=pltpu.SMEM),
            vmem,
            vmem,
            vmem,
            pl.BlockSpec((384, 512), lambda x: (0, x)),
        ],
        out_specs=pl.BlockSpec((384, 1024), lambda x: (0, x)),
        compiler_params=pltpu.CompilerParams(vmem_limit_bytes=48 << 20),
        cost_estimate=pl.CostEstimate(
            flops=2 * 384 * 2048 * 1024, bytes_accessed=9 << 20, transcendentals=0
        ),
    )(where, cot, kept, host, got)


def finish_kernel(norm_factor, s_ref, mine_ref, other_ref, m_ref, v_ref, m_out, v_out, step_out, host_out):
    is_mine = pl.program_id(0) == s_ref[0]
    for tile in range(8):
        y, half = tile // 2, tile % 2
        cols = slice(tile * 128, tile * 128 + 128)
        grad = norm_factor * jnp.where(
            is_mine, mine_ref[s_ref[1 + y], half], other_ref[s_ref[5 + y], half]
        ).T
        if tile < 5:
            moment = 0.9 * m_ref[:, cols] + 0.1 * grad
            second = 0.95 * v_ref[:, cols] + 0.05 * grad * grad
            m_out[:, cols] = moment
            v_out[:, cols] = second
            step_out[:, cols] = (
                moment / (1.0 - 0.9**20) / (jnp.sqrt(second / (1.0 - 0.95**20)) + 1e-08)
            )
        else:
            host_out[:, tile * 128 - 640 : tile * 128 - 512] = grad


def finish(norm_factor, where, mine, other, moment, second):
    vmem = pl.BlockSpec(memory_space=pltpu.VMEM)
    wide = pl.BlockSpec((128, 640), lambda i: (i, 0))
    return pl.pallas_call(
        functools.partial(finish_kernel, norm_factor),
        out_shape=(jax.ShapeDtypeStruct((256, 640), F32),) * 3 + (jax.ShapeDtypeStruct((256, 384), F32),),
        grid=(2,),
        in_specs=[pl.BlockSpec(memory_space=pltpu.SMEM), vmem, vmem, wide, wide],
        out_specs=(wide, wide, wide, pl.BlockSpec((128, 384), lambda i: (i, 0))),
        compiler_params=pltpu.CompilerParams(vmem_limit_bytes=32 << 20),
        cost_estimate=pl.CostEstimate(flops=1 << 22, bytes_accessed=6 << 20, transcendentals=0),
    )(where, mine, other, moment, second)


def has_host(c):
    return c["c"] == c["x"] + c["zl"] + c["zh"] & 1


def on_device(tokens, cotangent, weight, moment, second, delayed):
    me = where_am_i()
    device_cols = moment.shape[1]
    norm_factor = (tokens.shape[0] * lax.axis_size("rep") * lax.axis_size("fsdp")) ** (-0.5)
    y, zh, core = me["y"], me["zh"], me["c"]
    order = jnp.stack([core] + [at for axis in ("x", "zl", "y") for at in orders(me[axis], core)])
    order = order.astype(jnp.int32)
    host_places = lax.dynamic_slice(jnp.array(HOST_PLACES, jnp.int32), (zh * 4 + me["zl"], 0), (1, 4))
    where = jnp.stack([core] + places(me["x"], core) + places(me["zl"], core)).astype(jnp.int32)
    where = jnp.concatenate([where, host_places[0]])
    where_y = jnp.stack([core] + places(y, core) + places(y, 1 - core)).astype(jnp.int32)

    their_cot = send(cotangent, flip("c"))
    their_tokens = send(tokens, flip("c"))
    kept, refreshed = projection_rows(order, weight, delayed)
    kept_got = send(kept, partner("x", False))
    for_zh = send(
        refreshed,
        lambda c: dict(c, zh=1, zl=c["zl"] ^ 1) if c["y"] == c["zh"] == 0 and has_host(c) else None,
    )
    order, kept, kept_got = together(order, kept, kept_got)
    kept = jnp.stack([kept, kept_got])
    kept_got = send(kept, partner("x", True))
    order, kept = together(order, kept)
    one_out, two_out = chip_gradient(False, order, tokens, their_tokens, cotangent, their_cot)
    one_out, two_out, order, kept, kept_got, refreshed, for_zh = together(
        one_out, two_out, order, kept, kept_got, refreshed, for_zh
    )

    one_got = send(one_out, partner("x", True))
    two_got = send(two_out, partner("y", True))
    kept = jnp.concatenate([kept, kept_got])
    kept_a = send(kept, partner("zl", True))
    kept_b = send(kept, partner("zl", False))
    refreshed = jnp.where(zh == 0, refreshed, for_zh)
    first = core == (me["x"] + me["zl"] + zh) % 2
    lower, upper = refreshed[:, :128], refreshed[:, 128:]
    for_core = send(
        jnp.where(core == 0, upper, lower),
        lambda c: dict(c, c=1 - c["c"]) if c["y"] == 0 and has_host(c) else None,
    )
    one_held, two_held = chip_gradient(True, order, tokens, their_tokens, cotangent, their_cot)
    one_far = (one_held[0] + one_got[0].astype(F32)).astype(BF16)
    two_far = (two_held[0] + two_got[0].astype(F32)).astype(BF16)
    host = jnp.where(first, jnp.where(core == 0, lower, upper), for_core)
    one_far, two_far, kept, kept_a, kept_b, host = together(
        one_far, two_far, kept, kept_a, kept_b, host
    )

    one_got2 = send(one_far, partner("x", False))
    two_got2, host_got = ride(two_far, host, partner("y", False))
    kept_c = send(kept_b, partner("zl", True))
    one = one_held[1] + one_got[1].astype(F32) + one_got2.astype(F32)
    two = two_held[1] + two_got[1].astype(F32) + two_got2.astype(F32)
    host = jnp.where(y == jnp.where(core == 0, 3, 1), host_got, host)
    one, two, host, kept_c = together(one, two, host, kept_c)

    one_got, host_got = ride(one[:2].astype(BF16), host, partner("y", True))
    two_got = send(two[:2].astype(BF16), partner("x", True))
    one_far = (one[2] + one_got[0].astype(F32)).astype(BF16)
    two_far = (two[2] + two_got[0].astype(F32)).astype(BF16)
    host = jnp.where((y == 2) | (y == jnp.where(core == 0, 1, 3)), host_got, host)
    one_far, two_far, host = together(one_far, two_far, host)

    one_got2 = send(one_far, partner("y", False))
    two_got2 = send(two_far, partner("x", False))
    host_got = send(host, neighbour("zl", 1))
    both = jnp.stack(
        [
            one[3] + one_got[1].astype(F32) + one_got2.astype(F32),
            two[3] + two_got[1].astype(F32) + two_got2.astype(F32),
        ],
        axis=1,
    )
    both, host, host_got = together(both, host, host_got)

    got = send(both[:2], partner("zl", True))
    host = jnp.stack([host, host_got])
    host_got = send(host, neighbour("zl", 3))
    kept = jnp.stack([kept, kept_b, kept_a, kept_c])
    far = both[2] + got[0]
    far, host, host_got, kept = together(far, host, host_got, kept)
    got2 = send(far, partner("zl", False))
    host = jnp.concatenate([host, host_got])
    host_got = send(host, partner("x", False))
    total = (both[3] + got[1] + got2).astype(BF16)
    total, host = together(total, host)
    zh_got = send(total, flip("zh"))
    host = jnp.stack([host, host_got])
    host_got = send(host, partner("x", True))
    total = total.astype(F32) + zh_got.astype(F32)
    mine_got = send(total, partner("y", False))
    mine = jnp.stack([total, mine_got])
    mine, host = together(mine, host)
    mine_got = send(mine, partner("y", True))

    host = jnp.concatenate([host, host_got])
    theirs = their_input_gradient(where, their_cot, kept, host)
    got = send(theirs, flip("c"))
    mine = jnp.concatenate([mine, mine_got])
    mine, theirs = together(mine, theirs)
    other = send(mine, flip("c"))
    grad_input = our_input_gradient(where, cotangent, kept, host, got)
    mine, grad_input = together(mine, grad_input)
    return (grad_input, *finish(norm_factor, where_y, mine, other, moment, second))


def solution(mesh):
    placed = (
        P(("rep", "fsdp"), None),
        P(("rep", "fsdp"), None),
        P("fsdp", None),
        P("fsdp", None),
        P("fsdp", None),
        P("rep", "fsdp", None),
    )
    return jax.shard_map(
        on_device,
        mesh=mesh,
        in_specs=placed,
        out_specs=(
            P(("rep", "fsdp"), None),
            P("fsdp", None),
            P("fsdp", None),
            P("fsdp", None),
            P("fsdp", None),
        ),
        check_vma=False,
    )
```

```python
import functools

import jax
import jax.numpy as jnp
from jax import lax
from jax.experimental import pallas as pl
from jax.experimental.pallas import tpu as pltpu
from jax.sharding import PartitionSpec as P

AXES = ("rep", "fsdp")
SIZES = {"y": 4, "zh": 2, "c": 2, "x": 4, "zl": 4}
HOST_PLACES = (
    (0, 1, 2, 3),
    (1, 0, 2, 3),
    (3, 2, 0, 1),
    (3, 2, 1, 0),
    (1, 0, 3, 2),
    (0, 1, 3, 2),
    (2, 3, 1, 0),
    (2, 3, 0, 1),
)
F32 = jnp.float32
BF16 = jnp.bfloat16


def unflatten(i):
    c = {}
    for name in ("zl", "x", "c", "zh", "y"):
        c[name] = i % SIZES[name]
        i //= SIZES[name]
    c["c"] ^= c["x"] + c["y"] + c["zl"] & 1
    return c


def flatten(c):
    c = dict(c, c=c["c"] ^ (c["x"] + c["y"] + c["zl"] & 1))
    i = 0
    for name in ("y", "zh", "c", "x", "zl"):
        i = i * SIZES[name] + c[name]
    return i


def send(value, route):
    pairs = []
    for i in range(256):
        target = route(unflatten(i))
        if target is not None:
            pairs.append((i, flatten(target)))
    return lax.ppermute(value, AXES, pairs)


def neighbour(axis, mask):
    def route(c):
        t = dict(c)
        t[axis] = c[axis] ^ mask
        if axis == "zl" and mask == 3 and c["zl"] in (0, 3):
            t["zh"] = 1 - c["zh"]
        return t

    return route


def partner(axis, first):
    def route(c):
        return neighbour(axis, 1 if (c["c"] == 0) == first else 3)(c)

    return route


def flip(axis):
    def route(c):
        t = dict(c)
        t[axis] = 1 - c[axis]
        return t

    return route


def where_am_i():
    rep, fsdp = lax.axis_index("rep"), lax.axis_index("fsdp")
    y, x, zl = rep // 4, fsdp // 4, fsdp % 4
    return {"y": y, "zh": rep // 2 % 2, "c": rep % 2 ^ (x + y + zl) % 2, "x": x, "zl": zl}


def together(*values):
    return lax.optimization_barrier(values)


def places(p, core):
    b = jnp.where(core == 0, 3, 1)
    out = []
    for j in range(4):
        r = p ^ j
        out.append(jnp.where(r == 0, 0, jnp.where(r == b, 1, jnp.where(r == 2, 3, 2))))
    return out


def orders(p, core):
    a = jnp.where(core == 0, 1, 3)
    return [p ^ 2, p ^ a, p ^ a ^ 2, p]


def chosen(s_ref, t_ref):
    cuts = [pl.multiple_of(s_ref[5 + k] * 256 + s_ref[0] * 128, 128) for k in range(4)]
    return jnp.concatenate([t_ref[:, pl.ds(cut, 128)] for cut in cuts], axis=1)


def columns(s_ref, c_ref, half, places):
    cuts = [pl.multiple_of(s_ref[9 + y] * 256 + half * 128, 128) for y in places]
    return jnp.concatenate([c_ref[:, pl.ds(cut, 128)] for cut in cuts], axis=1).T


def grad_kernel(keep, s_ref, t_hbm, u_hbm, c_hbm, d_hbm, one_ref, two_ref, t, u, c, d, sems):
    places = (2, 3) if keep else (0, 1)
    loads = [pltpu.make_async_copy(c_hbm, c, sems.at[0]), pltpu.make_async_copy(d_hbm, d, sems.at[1])]
    for i in range(4):
        cut = pl.ds(pl.multiple_of(s_ref[1 + i] * 1024, 1024), 1024)
        loads.append(pltpu.make_async_copy(t_hbm.at[:, cut], t.at[i], sems.at[2 + 2 * i]))
        loads.append(pltpu.make_async_copy(u_hbm.at[:, cut], u.at[i], sems.at[3 + 2 * i]))
    for load in loads:
        load.start()
    for load in loads[:2]:
        load.wait()
    one_cot = jnp.concatenate([columns(s_ref, r, 0, range(4)) for r in (c, d)], axis=1)
    two_cot = jnp.concatenate([columns(s_ref, r, 1, places) for r in (c, d)], axis=1)
    for i in range(4):
        for load in loads[2 + 2 * i : 4 + 2 * i]:
            load.wait()
        rows = jnp.concatenate([chosen(s_ref, r) for r in (t.at[i], u.at[i])], axis=0)
        if i in places:
            total = jnp.dot(one_cot, rows, preferred_element_type=F32).astype(one_ref.dtype)
            for y in range(4):
                for k in range(4):
                    one_ref[i - places[0], y, k] = total[y * 128 : y * 128 + 128, k * 128 : k * 128 + 128]
        total = jnp.dot(two_cot, rows, preferred_element_type=F32).astype(two_ref.dtype)
        for y in range(2):
            for k in range(4):
                two_ref[y, i, k] = total[y * 128 : y * 128 + 128, k * 128 : k * 128 + 128]


def chip_gradient(keep, order, tokens, their_tokens, cot, their_cot):
    dtype = F32 if keep else BF16
    vmem = pl.BlockSpec(memory_space=pltpu.VMEM)
    return pl.pallas_call(
        functools.partial(grad_kernel, keep),
        out_shape=(jax.ShapeDtypeStruct((2, 4, 4, 128, 128), dtype),) * 2,
        in_specs=[pl.BlockSpec(memory_space=pltpu.SMEM)] + [pl.BlockSpec(memory_space=pl.ANY)] * 4,
        out_specs=[vmem] * 2,
        scratch_shapes=[pltpu.VMEM((4, 384, 1024), BF16)] * 2
        + [pltpu.VMEM((384, 1024), BF16)] * 2
        + [pltpu.SemaphoreType.DMA((10,))],
        compiler_params=pltpu.CompilerParams(vmem_limit_bytes=56 << 20),
        cost_estimate=pl.CostEstimate(
            flops=768 * 2048 * 1024, bytes_accessed=9 << 20, transcendentals=0
        ),
    )(order, tokens, their_tokens, cot, their_cot)


def kept_kernel(s_ref, w_ref, o_ref):
    mine = pl.ds(pl.multiple_of(s_ref[0] * 128, 128), 128)
    o_ref[...] = w_ref[mine, :640].T


def refreshed_kernel(w_ref, d_ref, o_ref):
    o_ref[...] = (w_ref[:, 640:].astype(F32) + d_ref[0]).astype(BF16).T


def rows_call(kernel, shape, *args):
    vmem, smem = pl.BlockSpec(memory_space=pltpu.VMEM), pl.BlockSpec(memory_space=pltpu.SMEM)
    return pl.pallas_call(
        kernel,
        out_shape=jax.ShapeDtypeStruct(shape, BF16),
        in_specs=[smem if arg.ndim == 1 else vmem for arg in args],
        out_specs=vmem,
        compiler_params=pltpu.CompilerParams(vmem_limit_bytes=16 << 20),
        cost_estimate=pl.CostEstimate(flops=1 << 17, bytes_accessed=1 << 20, transcendentals=0),
    )(*args)


def product(s_ref, cot_ref, w_ref, r_ref, at):
    width = w_ref.shape[-2]
    kept = jnp.concatenate([w_ref[s_ref[5 + zl], at] for zl in range(4)], axis=1)
    host = jnp.concatenate([r_ref[at, s_ref[9 + zl]] for zl in range(4)], axis=1)
    total = jnp.dot(cot_ref[:, :width], kept, preferred_element_type=F32)
    total += jnp.dot(cot_ref[:, width:], host, preferred_element_type=F32)
    return total.astype(BF16)


def theirs_kernel(s_ref, cot_ref, w_ref, r_ref, o_ref):
    for x in range(4):
        at = s_ref[1 + x]
        o_ref[:, x * 512 : x * 512 + 512] = product(s_ref, cot_ref, w_ref, r_ref, at)


def ours_kernel(s_ref, cot_ref, w_ref, r_ref, got_ref, o_ref):
    core = s_ref[0]
    total = product(s_ref, cot_ref, w_ref, r_ref, s_ref[1 + pl.program_id(0)])
    for zl in range(4):
        mine = pl.multiple_of(zl * 256 + core * 128, 128)
        other = pl.multiple_of(zl * 256 + 128 - core * 128, 128)
        o_ref[:, pl.ds(mine, 128)] = total[:, zl * 128 : zl * 128 + 128]
        o_ref[:, pl.ds(other, 128)] = got_ref[:, zl * 128 : zl * 128 + 128]


def their_input_gradient(where, cot, kept, host):
    vmem = pl.BlockSpec(memory_space=pltpu.VMEM)
    return pl.pallas_call(
        theirs_kernel,
        out_shape=jax.ShapeDtypeStruct((384, 2048), BF16),
        in_specs=[pl.BlockSpec(memory_space=pltpu.SMEM), vmem, vmem, vmem],
        out_specs=vmem,
        compiler_params=pltpu.CompilerParams(vmem_limit_bytes=32 << 20),
        cost_estimate=pl.CostEstimate(
            flops=6 * 384 * 2048 * 1024, bytes_accessed=12 << 20, transcendentals=0
        ),
    )(where, cot, kept, host)


def our_input_gradient(where, cot, kept, host, got):
    vmem = pl.BlockSpec(memory_space=pltpu.VMEM)
    return pl.pallas_call(
        ours_kernel,
        out_shape=jax.ShapeDtypeStruct((384, 4096), BF16),
        grid=(4,),
        in_specs=[
            pl.BlockSpec(memory_space=pltpu.SMEM),
            vmem,
            vmem,
            vmem,
            pl.BlockSpec((384, 512), lambda x: (0, x)),
        ],
        out_specs=pl.BlockSpec((384, 1024), lambda x: (0, x)),
        compiler_params=pltpu.CompilerParams(vmem_limit_bytes=36 << 20),
        cost_estimate=pl.CostEstimate(
            flops=2 * 384 * 2048 * 1024, bytes_accessed=9 << 20, transcendentals=0
        ),
    )(where, cot, kept, host, got)


def finish_kernel(norm_factor, s_ref, mine_ref, other_ref, m_ref, v_ref, m_out, v_out, step_out, host_out):
    is_mine = pl.program_id(0) == s_ref[0]
    for tile in range(8):
        y, half = tile // 2, tile % 2
        cols = slice(tile * 128, tile * 128 + 128)
        grad = norm_factor * jnp.where(
            is_mine, mine_ref[s_ref[1 + y], half], other_ref[s_ref[5 + y], half]
        ).T
        if tile < 5:
            moment = 0.9 * m_ref[:, cols] + 0.1 * grad
            second = 0.95 * v_ref[:, cols] + 0.05 * grad * grad
            m_out[:, cols] = moment
            v_out[:, cols] = second
            step_out[:, cols] = (
                moment / (1.0 - 0.9**20) / (jnp.sqrt(second / (1.0 - 0.95**20)) + 1e-08)
            )
        else:
            host_out[:, tile * 128 - 640 : tile * 128 - 512] = grad


def finish(norm_factor, where, mine, other, moment, second):
    vmem = pl.BlockSpec(memory_space=pltpu.VMEM)
    wide = pl.BlockSpec((128, 640), lambda i: (i, 0))
    return pl.pallas_call(
        functools.partial(finish_kernel, norm_factor),
        out_shape=(jax.ShapeDtypeStruct((256, 640), F32),) * 3 + (jax.ShapeDtypeStruct((256, 384), F32),),
        grid=(2,),
        in_specs=[pl.BlockSpec(memory_space=pltpu.SMEM), vmem, vmem, wide, wide],
        out_specs=(wide, wide, wide, pl.BlockSpec((128, 384), lambda i: (i, 0))),
        compiler_params=pltpu.CompilerParams(vmem_limit_bytes=32 << 20),
        cost_estimate=pl.CostEstimate(flops=1 << 22, bytes_accessed=6 << 20, transcendentals=0),
    )(where, mine, other, moment, second)


def has_host(c):
    return c["c"] == c["x"] + c["zl"] + c["zh"] & 1


def on_device(tokens, cotangent, weight, moment, second, delayed):
    me = where_am_i()
    device_cols = moment.shape[1]
    norm_factor = (tokens.shape[0] * lax.axis_size("rep") * lax.axis_size("fsdp")) ** (-0.5)
    y, zh, core = me["y"], me["zh"], me["c"]
    order = jnp.stack([core] + [at for axis in ("x", "zl", "y") for at in orders(me[axis], core)])
    order = order.astype(jnp.int32)
    host_places = lax.dynamic_slice(jnp.array(HOST_PLACES, jnp.int32), (zh * 4 + me["zl"], 0), (1, 4))
    where = jnp.stack([core] + places(me["x"], core) + places(me["zl"], core)).astype(jnp.int32)
    where = jnp.concatenate([where, host_places[0]])
    where_y = jnp.stack([core] + places(y, core) + places(y, 1 - core)).astype(jnp.int32)

    their_cot = send(cotangent, flip("c"))
    their_tokens = send(tokens, flip("c"))
    kept = rows_call(kept_kernel, (640, 128), order, weight)
    refreshed = rows_call(refreshed_kernel, (384, 256), weight, delayed)
    for_zh = send(
        refreshed,
        lambda c: dict(c, zh=1, zl=c["zl"] ^ 1) if c["y"] == c["zh"] == 0 and has_host(c) else None,
    )
    kept_got = send(kept, partner("x", False))
    order, kept, kept_got, refreshed = together(order, kept, kept_got, refreshed)
    kept = jnp.stack([kept, kept_got])
    kept_got = send(kept, partner("x", True))
    order, kept = together(order, kept)
    one_out, two_out = chip_gradient(False, order, tokens, their_tokens, cotangent, their_cot)
    one_out, two_out, order, kept, kept_got, refreshed, for_zh = together(
        one_out, two_out, order, kept, kept_got, refreshed, for_zh
    )

    one_got = send(one_out, partner("x", True))
    two_got = send(two_out, partner("y", True))
    kept = jnp.concatenate([kept, kept_got])
    kept_a = send(kept, partner("zl", True))
    kept_b = send(kept, partner("zl", False))
    refreshed = jnp.where(zh == 0, refreshed, for_zh)
    first = core == (me["x"] + me["zl"] + zh) % 2
    lower, upper = refreshed[:, :128], refreshed[:, 128:]
    for_core = send(
        jnp.where(core == 0, upper, lower),
        lambda c: dict(c, c=1 - c["c"]) if c["y"] == 0 and has_host(c) else None,
    )
    one_held, two_held = chip_gradient(True, order, tokens, their_tokens, cotangent, their_cot)
    one_held, two_held, one_got, two_got = together(one_held, two_held, one_got, two_got)
    one_far = (one_held[0] + one_got[0].astype(F32)).astype(BF16)
    two_far = (two_held[0] + two_got[0].astype(F32)).astype(BF16)
    host = jnp.where(first, jnp.where(core == 0, lower, upper), for_core)
    one_far, two_far, kept, kept_a, kept_b, host = together(
        one_far, two_far, kept, kept_a, kept_b, host
    )

    one_got2 = send(one_far, partner("x", False))
    two_got2 = send(two_far, partner("y", False))
    by_y = [send(host, lambda c, k=k: dict(c, y=k) if c["y"] == 0 else None) for k in (1, 3, 2)]
    kept_c = send(kept_b, partner("zl", True))
    one = one_held[1] + one_got[1].astype(F32) + one_got2.astype(F32)
    two = two_held[1] + two_got[1].astype(F32) + two_got2.astype(F32)
    host = jnp.where(y == 0, host, jnp.where(y == 1, by_y[0], jnp.where(y == 3, by_y[1], by_y[2])))
    one, two, host, kept_c = together(one, two, host, kept_c)

    one_got = send(one[:2].astype(BF16), partner("y", True))
    host_got = send(host, neighbour("zl", 1))
    two_got = send(two[:2].astype(BF16), partner("x", True))
    one_far = (one[2] + one_got[0].astype(F32)).astype(BF16)
    two_far = (two[2] + two_got[0].astype(F32)).astype(BF16)
    one_far, two_far, host, host_got = together(one_far, two_far, host, host_got)

    one_got2 = send(one_far, partner("y", False))
    two_got2 = send(two_far, partner("x", False))
    host = jnp.stack([host, host_got])
    host_got = send(host, neighbour("zl", 3))
    both = jnp.stack(
        [
            one[3] + one_got[1].astype(F32) + one_got2.astype(F32),
            two[3] + two_got[1].astype(F32) + two_got2.astype(F32),
        ],
        axis=1,
    )
    both, host, host_got = together(both, host, host_got)

    got = send(both[:2], partner("zl", True))
    host = jnp.concatenate([host, host_got])
    host_got = send(host, partner("x", False))
    kept = jnp.stack([kept, kept_b, kept_a, kept_c])
    far = both[2] + got[0]
    far, host, host_got, kept = together(far, host, host_got, kept)
    got2 = send(far, partner("zl", False))
    host = jnp.stack([host, host_got])
    host_got = send(host, partner("x", True))
    total = (both[3] + got[1] + got2).astype(BF16)
    total, host = together(total, host)
    zh_got = send(total, flip("zh"))

    host = jnp.concatenate([host, host_got])
    theirs = their_input_gradient(where, their_cot, kept, host)
    total, zh_got, theirs = together(total, zh_got, theirs)
    got = send(theirs, flip("c"))
    total = total.astype(F32) + zh_got.astype(F32)
    mine = jnp.stack([total, send(total, partner("y", False))])
    mine_got = send(mine, partner("y", True))
    grad_input = our_input_gradient(where, cotangent, kept, host, got)
    mine, mine_got, grad_input = together(mine, mine_got, grad_input)
    mine = jnp.concatenate([mine, mine_got])
    other = send(mine, flip("c"))
    return (grad_input, *finish(norm_factor, where_y, mine, other, moment, second))


def solution(mesh):
    placed = (
        P(("rep", "fsdp"), None),
        P(("rep", "fsdp"), None),
        P("fsdp", None),
        P("fsdp", None),
        P("fsdp", None),
        P("rep", "fsdp", None),
    )
    return jax.shard_map(
        on_device,
        mesh=mesh,
        in_specs=placed,
        out_specs=(
            P(("rep", "fsdp"), None),
            P("fsdp", None),
            P("fsdp", None),
            P("fsdp", None),
            P("fsdp", None),
        ),
        check_vma=False,
    )
```

```python
import functools

import jax
import jax.numpy as jnp
from jax import lax
from jax.experimental import pallas as pl
from jax.experimental.pallas import tpu as pltpu
from jax.sharding import PartitionSpec as P

AXES = ("rep", "fsdp")
SIZES = {"y": 4, "zh": 2, "c": 2, "x": 4, "zl": 4}
HOST_PLACES = (
    (0, 1, 2, 3),
    (1, 0, 2, 3),
    (3, 2, 0, 1),
    (3, 2, 1, 0),
    (1, 0, 3, 2),
    (0, 1, 3, 2),
    (2, 3, 1, 0),
    (2, 3, 0, 1),
)
F32 = jnp.float32
BF16 = jnp.bfloat16


def unflatten(i):
    c = {}
    for name in ("zl", "x", "c", "zh", "y"):
        c[name] = i % SIZES[name]
        i //= SIZES[name]
    c["c"] ^= c["x"] + c["y"] + c["zl"] & 1
    return c


def flatten(c):
    c = dict(c, c=c["c"] ^ (c["x"] + c["y"] + c["zl"] & 1))
    i = 0
    for name in ("y", "zh", "c", "x", "zl"):
        i = i * SIZES[name] + c[name]
    return i


def send(value, route):
    pairs = []
    for i in range(256):
        target = route(unflatten(i))
        if target is not None:
            pairs.append((i, flatten(target)))
    return lax.ppermute(value, AXES, pairs)


def neighbour(axis, mask):
    def route(c):
        t = dict(c)
        t[axis] = c[axis] ^ mask
        if axis == "zl" and mask == 3 and c["zl"] in (0, 3):
            t["zh"] = 1 - c["zh"]
        return t

    return route


def partner(axis, first):
    def route(c):
        return neighbour(axis, 1 if (c["c"] == 0) == first else 3)(c)

    return route


def flip(axis):
    def route(c):
        t = dict(c)
        t[axis] = 1 - c[axis]
        return t

    return route


def where_am_i():
    rep, fsdp = lax.axis_index("rep"), lax.axis_index("fsdp")
    y, x, zl = rep // 4, fsdp // 4, fsdp % 4
    return {"y": y, "zh": rep // 2 % 2, "c": rep % 2 ^ (x + y + zl) % 2, "x": x, "zl": zl}


def together(*values):
    return lax.optimization_barrier(values)


def places(p, core):
    b = jnp.where(core == 0, 3, 1)
    out = []
    for j in range(4):
        r = p ^ j
        out.append(jnp.where(r == 0, 0, jnp.where(r == b, 1, jnp.where(r == 2, 3, 2))))
    return out


def orders(p, core):
    a = jnp.where(core == 0, 1, 3)
    return [p ^ 2, p ^ a, p ^ a ^ 2, p]


def chosen(s_ref, t_ref):
    cuts = [pl.multiple_of(s_ref[5 + k] * 256 + s_ref[0] * 128, 128) for k in range(4)]
    return jnp.concatenate([t_ref[:, pl.ds(cut, 128)] for cut in cuts], axis=1)


def columns(s_ref, c_ref, half, places):
    cuts = [pl.multiple_of(s_ref[9 + y] * 256 + half * 128, 128) for y in places]
    return jnp.concatenate([c_ref[:, pl.ds(cut, 128)] for cut in cuts], axis=1).T


def grad_kernel(keep, s_ref, t_hbm, u_hbm, c_hbm, d_hbm, one_ref, two_ref, t, u, c, d, sems):
    places = (2, 3) if keep else (0, 1)
    loads = [pltpu.make_async_copy(c_hbm, c, sems.at[0]), pltpu.make_async_copy(d_hbm, d, sems.at[1])]
    for i in range(4):
        cut = pl.ds(pl.multiple_of(s_ref[1 + i] * 1024, 1024), 1024)
        loads.append(pltpu.make_async_copy(t_hbm.at[:, cut], t.at[i], sems.at[2 + 2 * i]))
        loads.append(pltpu.make_async_copy(u_hbm.at[:, cut], u.at[i], sems.at[3 + 2 * i]))
    for load in loads:
        load.start()
    for load in loads[:2]:
        load.wait()
    one_cot = jnp.concatenate([columns(s_ref, r, 0, range(4)) for r in (c, d)], axis=1)
    two_cot = jnp.concatenate([columns(s_ref, r, 1, places) for r in (c, d)], axis=1)
    for i in range(4):
        for load in loads[2 + 2 * i : 4 + 2 * i]:
            load.wait()
        rows = jnp.concatenate([chosen(s_ref, r) for r in (t.at[i], u.at[i])], axis=0)
        if i in places:
            total = jnp.dot(one_cot, rows, preferred_element_type=F32).astype(one_ref.dtype)
            for y in range(4):
                for k in range(4):
                    one_ref[i - places[0], y, k] = total[y * 128 : y * 128 + 128, k * 128 : k * 128 + 128]
        total = jnp.dot(two_cot, rows, preferred_element_type=F32).astype(two_ref.dtype)
        for y in range(2):
            for k in range(4):
                two_ref[y, i, k] = total[y * 128 : y * 128 + 128, k * 128 : k * 128 + 128]


def chip_gradient(keep, order, tokens, their_tokens, cot, their_cot):
    dtype = F32 if keep else BF16
    vmem = pl.BlockSpec(memory_space=pltpu.VMEM)
    return pl.pallas_call(
        functools.partial(grad_kernel, keep),
        out_shape=(jax.ShapeDtypeStruct((2, 4, 4, 128, 128), dtype),) * 2,
        in_specs=[pl.BlockSpec(memory_space=pltpu.SMEM)] + [pl.BlockSpec(memory_space=pl.ANY)] * 4,
        out_specs=[vmem] * 2,
        scratch_shapes=[pltpu.VMEM((4, 384, 1024), BF16)] * 2
        + [pltpu.VMEM((384, 1024), BF16)] * 2
        + [pltpu.SemaphoreType.DMA((10,))],
        compiler_params=pltpu.CompilerParams(vmem_limit_bytes=56 << 20),
        cost_estimate=pl.CostEstimate(
            flops=768 * 2048 * 1024, bytes_accessed=9 << 20, transcendentals=0
        ),
    )(order, tokens, their_tokens, cot, their_cot)


def kept_kernel(s_ref, w_ref, o_ref):
    mine = pl.ds(pl.multiple_of(s_ref[0] * 128, 128), 128)
    o_ref[...] = w_ref[mine, :640].T


def refreshed_kernel(w_ref, d_ref, o_ref):
    o_ref[...] = (w_ref[:, 640:].astype(F32) + d_ref[0]).astype(BF16).T


def rows_call(kernel, shape, *args):
    vmem, smem = pl.BlockSpec(memory_space=pltpu.VMEM), pl.BlockSpec(memory_space=pltpu.SMEM)
    return pl.pallas_call(
        kernel,
        out_shape=jax.ShapeDtypeStruct(shape, BF16),
        in_specs=[smem if arg.ndim == 1 else vmem for arg in args],
        out_specs=vmem,
        compiler_params=pltpu.CompilerParams(vmem_limit_bytes=16 << 20),
        cost_estimate=pl.CostEstimate(flops=1 << 17, bytes_accessed=1 << 20, transcendentals=0),
    )(*args)


def product(s_ref, cot_ref, w_ref, r_ref, at):
    width = w_ref.shape[-2]
    kept = jnp.concatenate([w_ref[s_ref[5 + zl], at] for zl in range(4)], axis=1)
    host = jnp.concatenate([r_ref[at, s_ref[9 + zl]] for zl in range(4)], axis=1)
    total = jnp.dot(cot_ref[:, :width], kept, preferred_element_type=F32)
    total += jnp.dot(cot_ref[:, width:], host, preferred_element_type=F32)
    return total.astype(BF16)


def theirs_kernel(s_ref, cot_ref, w_ref, r_ref, o_ref):
    for x in range(4):
        at = s_ref[1 + x]
        o_ref[:, x * 512 : x * 512 + 512] = product(s_ref, cot_ref, w_ref, r_ref, at)


def ours_kernel(s_ref, cot_ref, w_ref, r_ref, got_ref, o_ref):
    core = s_ref[0]
    total = product(s_ref, cot_ref, w_ref, r_ref, s_ref[1 + pl.program_id(0)])
    for zl in range(4):
        mine = pl.multiple_of(zl * 256 + core * 128, 128)
        other = pl.multiple_of(zl * 256 + 128 - core * 128, 128)
        o_ref[:, pl.ds(mine, 128)] = total[:, zl * 128 : zl * 128 + 128]
        o_ref[:, pl.ds(other, 128)] = got_ref[:, zl * 128 : zl * 128 + 128]


def their_input_gradient(where, cot, kept, host):
    vmem = pl.BlockSpec(memory_space=pltpu.VMEM)
    return pl.pallas_call(
        theirs_kernel,
        out_shape=jax.ShapeDtypeStruct((384, 2048), BF16),
        in_specs=[pl.BlockSpec(memory_space=pltpu.SMEM), vmem, vmem, vmem],
        out_specs=vmem,
        compiler_params=pltpu.CompilerParams(vmem_limit_bytes=32 << 20),
        cost_estimate=pl.CostEstimate(
            flops=6 * 384 * 2048 * 1024, bytes_accessed=12 << 20, transcendentals=0
        ),
    )(where, cot, kept, host)


def our_input_gradient(where, cot, kept, host, got):
    vmem = pl.BlockSpec(memory_space=pltpu.VMEM)
    return pl.pallas_call(
        ours_kernel,
        out_shape=jax.ShapeDtypeStruct((384, 4096), BF16),
        grid=(4,),
        in_specs=[
            pl.BlockSpec(memory_space=pltpu.SMEM),
            vmem,
            vmem,
            vmem,
            pl.BlockSpec((384, 512), lambda x: (0, x)),
        ],
        out_specs=pl.BlockSpec((384, 1024), lambda x: (0, x)),
        compiler_params=pltpu.CompilerParams(vmem_limit_bytes=36 << 20),
        cost_estimate=pl.CostEstimate(
            flops=2 * 384 * 2048 * 1024, bytes_accessed=9 << 20, transcendentals=0
        ),
    )(where, cot, kept, host, got)


def finish_kernel(norm_factor, s_ref, mine_ref, other_ref, m_ref, v_ref, m_out, v_out, step_out, host_out):
    is_mine = pl.program_id(0) == s_ref[0]
    for tile in range(8):
        y, half = tile // 2, tile % 2
        cols = slice(tile * 128, tile * 128 + 128)
        grad = norm_factor * jnp.where(
            is_mine, mine_ref[s_ref[1 + y], half], other_ref[s_ref[5 + y], half]
        ).T
        if tile < 5:
            moment = 0.9 * m_ref[:, cols] + 0.1 * grad
            second = 0.95 * v_ref[:, cols] + 0.05 * grad * grad
            m_out[:, cols] = moment
            v_out[:, cols] = second
            step_out[:, cols] = (
                moment / (1.0 - 0.9**20) / (jnp.sqrt(second / (1.0 - 0.95**20)) + 1e-08)
            )
        else:
            host_out[:, tile * 128 - 640 : tile * 128 - 512] = grad


def finish(norm_factor, where, mine, other, moment, second):
    vmem = pl.BlockSpec(memory_space=pltpu.VMEM)
    wide = pl.BlockSpec((128, 640), lambda i: (i, 0))
    return pl.pallas_call(
        functools.partial(finish_kernel, norm_factor),
        out_shape=(jax.ShapeDtypeStruct((256, 640), F32),) * 3 + (jax.ShapeDtypeStruct((256, 384), F32),),
        grid=(2,),
        in_specs=[pl.BlockSpec(memory_space=pltpu.SMEM), vmem, vmem, wide, wide],
        out_specs=(wide, wide, wide, pl.BlockSpec((128, 384), lambda i: (i, 0))),
        compiler_params=pltpu.CompilerParams(vmem_limit_bytes=32 << 20),
        cost_estimate=pl.CostEstimate(flops=1 << 22, bytes_accessed=6 << 20, transcendentals=0),
    )(where, mine, other, moment, second)


def on_device(tokens, cotangent, weight, moment, second, delayed):
    me = where_am_i()
    device_cols = moment.shape[1]
    norm_factor = (tokens.shape[0] * lax.axis_size("rep") * lax.axis_size("fsdp")) ** (-0.5)
    y, zh, core = me["y"], me["zh"], me["c"]
    order = jnp.stack([core] + [at for axis in ("x", "zl", "y") for at in orders(me[axis], core)])
    order = order.astype(jnp.int32)
    host_places = lax.dynamic_slice(jnp.array(HOST_PLACES, jnp.int32), (zh * 4 + me["zl"], 0), (1, 4))
    where = jnp.stack([core] + places(me["x"], core) + places(me["zl"], core)).astype(jnp.int32)
    where = jnp.concatenate([where, host_places[0]])
    where_y = jnp.stack([core] + places(y, core) + places(y, 1 - core)).astype(jnp.int32)

    their_cot = send(cotangent, flip("c"))
    their_tokens = send(tokens, flip("c"))
    kept = rows_call(kept_kernel, (640, 128), order, weight)
    refreshed = rows_call(refreshed_kernel, (384, 256), weight, delayed)
    lower, upper = refreshed[:, :128], refreshed[:, 128:]
    host_got = send(
        jnp.where(core == 0, upper, lower),
        lambda c: dict(c, c=1 - c["c"]) if c["y"] == c["zh"] == 0 else None,
    )
    kept_got = send(kept, partner("x", False))
    order, kept, kept_got, lower, host_got = together(order, kept, kept_got, lower, host_got)
    on_root = core == (me["x"] + me["zl"]) % 2
    host = jnp.where(on_root, jnp.where(core == 0, lower, upper), host_got)
    host_got = send(
        host, lambda c: dict(c, zh=1, zl=c["zl"] ^ 1) if c["y"] == c["zh"] == 0 else None
    )
    kept = jnp.stack([kept, kept_got])
    kept_got = send(kept, partner("x", True))
    order, kept = together(order, kept)
    one_out, two_out = chip_gradient(False, order, tokens, their_tokens, cotangent, their_cot)
    one_out, two_out, order, kept, kept_got, host, host_got = together(
        one_out, two_out, order, kept, kept_got, host, host_got
    )

    one_got = send(one_out, partner("x", True))
    two_got = send(two_out, partner("y", True))
    kept = jnp.concatenate([kept, kept_got])
    kept_a = send(kept, partner("zl", True))
    kept_b = send(kept, partner("zl", False))
    host = jnp.where(zh == 0, host, host_got)
    host_got = send(host, partner("y", True))
    one_held, two_held = chip_gradient(True, order, tokens, their_tokens, cotangent, their_cot)
    one_held, two_held, one_got, two_got = together(one_held, two_held, one_got, two_got)
    one_far = (one_held[0] + one_got[0].astype(F32)).astype(BF16)
    two_far = (two_held[0] + two_got[0].astype(F32)).astype(BF16)
    host = jnp.where(y == jnp.where(core == 0, 1, 3), host_got, host)
    one_far, two_far, kept, kept_a, kept_b, host = together(
        one_far, two_far, kept, kept_a, kept_b, host
    )

    one_got2 = send(one_far, partner("x", False))
    two_got2 = send(two_far, partner("y", False))
    host_got = send(host, partner("y", False))
    kept_c = send(kept_b, partner("zl", True))
    one = one_held[1] + one_got[1].astype(F32) + one_got2.astype(F32)
    two = two_held[1] + two_got[1].astype(F32) + two_got2.astype(F32)
    host = jnp.where((y == 2) | (y == jnp.where(core == 0, 3, 1)), host_got, host)
    one, two, host, kept_c = together(one, two, host, kept_c)

    one_got = send(one[:2].astype(BF16), partner("y", True))
    host_got = send(host, neighbour("zl", 1))
    two_got = send(two[:2].astype(BF16), partner("x", True))
    one_far = (one[2] + one_got[0].astype(F32)).astype(BF16)
    two_far = (two[2] + two_got[0].astype(F32)).astype(BF16)
    one_far, two_far, host, host_got = together(one_far, two_far, host, host_got)

    one_got2 = send(one_far, partner("y", False))
    two_got2 = send(two_far, partner("x", False))
    host = jnp.stack([host, host_got])
    host_got = send(host, neighbour("zl", 3))
    one_got2, two_got2, host_got = together(one_got2, two_got2, host_got)
    both = jnp.stack(
        [
            one[3] + one_got[1].astype(F32) + one_got2.astype(F32),
            two[3] + two_got[1].astype(F32) + two_got2.astype(F32),
        ],
        axis=1,
    )
    both, host, host_got = together(both, host, host_got)

    got = send(both[:2], partner("zl", True))
    host = jnp.concatenate([host, host_got])
    host_got = send(host, partner("x", False))
    kept = jnp.stack([kept, kept_b, kept_a, kept_c])
    got, host, host_got, kept = together(got, host, host_got, kept)
    far = both[2] + got[0]
    got2 = send(far, partner("zl", False))
    host = jnp.stack([host, host_got])
    host_got = send(host, partner("x", True))
    total = (both[3] + got[1] + got2).astype(BF16)
    total, host = together(total, host)
    zh_got = send(total, flip("zh"))

    host = jnp.concatenate([host, host_got])
    theirs = their_input_gradient(where, their_cot, kept, host)
    total, zh_got, theirs = together(total, zh_got, theirs)
    got = send(theirs, flip("c"))
    total = total.astype(F32) + zh_got.astype(F32)
    mine = jnp.stack([total, send(total, partner("y", False))])
    mine_got = send(mine, partner("y", True))
    grad_input = our_input_gradient(where, cotangent, kept, host, got)
    mine, mine_got, grad_input = together(mine, mine_got, grad_input)
    mine = jnp.concatenate([mine, mine_got])
    other = send(mine, flip("c"))
    return (grad_input, *finish(norm_factor, where_y, mine, other, moment, second))


def solution(mesh):
    placed = (
        P(("rep", "fsdp"), None),
        P(("rep", "fsdp"), None),
        P("fsdp", None),
        P("fsdp", None),
        P("fsdp", None),
        P("rep", "fsdp", None),
    )
    return jax.shard_map(
        on_device,
        mesh=mesh,
        in_specs=placed,
        out_specs=(
            P(("rep", "fsdp"), None),
            P("fsdp", None),
            P("fsdp", None),
            P("fsdp", None),
            P("fsdp", None),
        ),
        check_vma=False,
    )
```

```python
import functools

import jax
import jax.numpy as jnp
from jax import lax
from jax.experimental import pallas as pl
from jax.experimental.pallas import tpu as pltpu
from jax.sharding import PartitionSpec as P

AXES = ("rep", "fsdp")
SIZES = {"y": 4, "zh": 2, "c": 2, "x": 4, "zl": 4}
HOST_PLACES = (
    (0, 1, 2, 3),
    (1, 0, 2, 3),
    (3, 2, 0, 1),
    (3, 2, 1, 0),
    (1, 0, 3, 2),
    (0, 1, 3, 2),
    (2, 3, 1, 0),
    (2, 3, 0, 1),
)
F32 = jnp.float32
BF16 = jnp.bfloat16


def unflatten(i):
    c = {}
    for name in ("zl", "x", "c", "zh", "y"):
        c[name] = i % SIZES[name]
        i //= SIZES[name]
    c["c"] ^= c["x"] + c["y"] + c["zl"] & 1
    return c


def flatten(c):
    c = dict(c, c=c["c"] ^ (c["x"] + c["y"] + c["zl"] & 1))
    i = 0
    for name in ("y", "zh", "c", "x", "zl"):
        i = i * SIZES[name] + c[name]
    return i


def send(value, route):
    pairs = []
    for i in range(256):
        target = route(unflatten(i))
        if target is not None:
            pairs.append((i, flatten(target)))
    return lax.ppermute(value, AXES, pairs)


def neighbour(axis, mask):
    def route(c):
        t = dict(c)
        t[axis] = c[axis] ^ mask
        if axis == "zl" and mask == 3 and c["zl"] in (0, 3):
            t["zh"] = 1 - c["zh"]
        return t

    return route


def partner(axis, first):
    def route(c):
        return neighbour(axis, 1 if (c["c"] == 0) == first else 3)(c)

    return route


def flip(axis):
    def route(c):
        t = dict(c)
        t[axis] = 1 - c[axis]
        return t

    return route


def where_am_i():
    rep, fsdp = lax.axis_index("rep"), lax.axis_index("fsdp")
    y, x, zl = rep // 4, fsdp // 4, fsdp % 4
    return {"y": y, "zh": rep // 2 % 2, "c": rep % 2 ^ (x + y + zl) % 2, "x": x, "zl": zl}


def together(*values):
    return lax.optimization_barrier(values)


def places(p, core):
    b = jnp.where(core == 0, 3, 1)
    out = []
    for j in range(4):
        r = p ^ j
        out.append(jnp.where(r == 0, 0, jnp.where(r == b, 1, jnp.where(r == 2, 3, 2))))
    return out


def orders(p, core):
    a = jnp.where(core == 0, 1, 3)
    return [p ^ 2, p ^ a, p ^ a ^ 2, p]


def chosen(s_ref, t_ref):
    cuts = [pl.multiple_of(s_ref[5 + k] * 256 + s_ref[0] * 128, 128) for k in range(4)]
    return jnp.concatenate([t_ref[:, pl.ds(cut, 128)] for cut in cuts], axis=1)


def columns(s_ref, c_ref, half, places):
    cuts = [pl.multiple_of(s_ref[9 + y] * 256 + half * 128, 128) for y in places]
    return jnp.concatenate([c_ref[:, pl.ds(cut, 128)] for cut in cuts], axis=1).T


def grad_kernel(keep, s_ref, t_hbm, u_hbm, c_hbm, d_hbm, one_ref, two_ref, t, u, c, d, sems):
    places = (2, 3) if keep else (0, 1)
    loads = [pltpu.make_async_copy(c_hbm, c, sems.at[0]), pltpu.make_async_copy(d_hbm, d, sems.at[1])]
    for i in range(4):
        cut = pl.ds(pl.multiple_of(s_ref[1 + i] * 1024, 1024), 1024)
        loads.append(pltpu.make_async_copy(t_hbm.at[:, cut], t.at[i], sems.at[2 + 2 * i]))
        loads.append(pltpu.make_async_copy(u_hbm.at[:, cut], u.at[i], sems.at[3 + 2 * i]))
    for load in loads:
        load.start()
    for load in loads[:2]:
        load.wait()
    one_cot = jnp.concatenate([columns(s_ref, r, 0, range(4)) for r in (c, d)], axis=1)
    two_cot = jnp.concatenate([columns(s_ref, r, 1, places) for r in (c, d)], axis=1)
    for i in range(4):
        for load in loads[2 + 2 * i : 4 + 2 * i]:
            load.wait()
        rows = jnp.concatenate([chosen(s_ref, r) for r in (t.at[i], u.at[i])], axis=0)
        if i in places:
            total = jnp.dot(one_cot, rows, preferred_element_type=F32).astype(one_ref.dtype)
            for y in range(4):
                for k in range(4):
                    one_ref[i - places[0], y, k] = total[y * 128 : y * 128 + 128, k * 128 : k * 128 + 128]
        total = jnp.dot(two_cot, rows, preferred_element_type=F32).astype(two_ref.dtype)
        for y in range(2):
            for k in range(4):
                two_ref[y, i, k] = total[y * 128 : y * 128 + 128, k * 128 : k * 128 + 128]


def chip_gradient(keep, order, tokens, their_tokens, cot, their_cot):
    dtype = F32 if keep else BF16
    vmem = pl.BlockSpec(memory_space=pltpu.VMEM)
    return pl.pallas_call(
        functools.partial(grad_kernel, keep),
        out_shape=(jax.ShapeDtypeStruct((2, 4, 4, 128, 128), dtype),) * 2,
        in_specs=[pl.BlockSpec(memory_space=pltpu.SMEM)] + [pl.BlockSpec(memory_space=pl.ANY)] * 4,
        out_specs=[vmem] * 2,
        scratch_shapes=[pltpu.VMEM((4, 384, 1024), BF16)] * 2
        + [pltpu.VMEM((384, 1024), BF16)] * 2
        + [pltpu.SemaphoreType.DMA((10,))],
        compiler_params=pltpu.CompilerParams(vmem_limit_bytes=(44 if keep else 56) << 20),
        cost_estimate=pl.CostEstimate(
            flops=768 * 2048 * 1024, bytes_accessed=9 << 20, transcendentals=0
        ),
    )(order, tokens, their_tokens, cot, their_cot)


def kept_kernel(s_ref, w_ref, o_ref):
    mine = pl.ds(pl.multiple_of(s_ref[0] * 128, 128), 128)
    o_ref[...] = w_ref[mine, :640].T


def refreshed_kernel(w_ref, d_ref, o_ref):
    o_ref[...] = (w_ref[:, 640:].astype(F32) + d_ref[0]).astype(BF16).T


def rows_call(kernel, shape, *args):
    vmem, smem = pl.BlockSpec(memory_space=pltpu.VMEM), pl.BlockSpec(memory_space=pltpu.SMEM)
    return pl.pallas_call(
        kernel,
        out_shape=jax.ShapeDtypeStruct(shape, BF16),
        in_specs=[smem if arg.ndim == 1 else vmem for arg in args],
        out_specs=vmem,
        compiler_params=pltpu.CompilerParams(vmem_limit_bytes=16 << 20),
        cost_estimate=pl.CostEstimate(flops=1 << 17, bytes_accessed=1 << 20, transcendentals=0),
    )(*args)


def product(s_ref, cot_ref, w_ref, r_ref, at):
    width = w_ref.shape[-2]
    kept = jnp.concatenate([w_ref[s_ref[5 + zl], at] for zl in range(4)], axis=1)
    host = jnp.concatenate([r_ref[at, s_ref[9 + zl]] for zl in range(4)], axis=1)
    total = jnp.dot(cot_ref[:, :width], kept, preferred_element_type=F32)
    total += jnp.dot(cot_ref[:, width:], host, preferred_element_type=F32)
    return total.astype(BF16)


def theirs_kernel(s_ref, cot_ref, w_ref, r_ref, o_ref):
    for x in range(4):
        at = s_ref[1 + x]
        o_ref[:, x * 512 : x * 512 + 512] = product(s_ref, cot_ref, w_ref, r_ref, at)


def ours_kernel(s_ref, cot_ref, w_ref, r_ref, got_ref, o_ref):
    core = s_ref[0]
    total = product(s_ref, cot_ref, w_ref, r_ref, s_ref[1 + pl.program_id(0)])
    for zl in range(4):
        mine = pl.multiple_of(zl * 256 + core * 128, 128)
        other = pl.multiple_of(zl * 256 + 128 - core * 128, 128)
        o_ref[:, pl.ds(mine, 128)] = total[:, zl * 128 : zl * 128 + 128]
        o_ref[:, pl.ds(other, 128)] = got_ref[:, zl * 128 : zl * 128 + 128]


def their_input_gradient(where, cot, kept, host):
    vmem = pl.BlockSpec(memory_space=pltpu.VMEM)
    return pl.pallas_call(
        theirs_kernel,
        out_shape=jax.ShapeDtypeStruct((384, 2048), BF16),
        in_specs=[pl.BlockSpec(memory_space=pltpu.SMEM), vmem, vmem, vmem],
        out_specs=vmem,
        compiler_params=pltpu.CompilerParams(vmem_limit_bytes=32 << 20),
        cost_estimate=pl.CostEstimate(
            flops=6 * 384 * 2048 * 1024, bytes_accessed=12 << 20, transcendentals=0
        ),
    )(where, cot, kept, host)


def our_input_gradient(where, cot, kept, host, got):
    vmem = pl.BlockSpec(memory_space=pltpu.VMEM)
    return pl.pallas_call(
        ours_kernel,
        out_shape=jax.ShapeDtypeStruct((384, 4096), BF16),
        grid=(4,),
        in_specs=[
            pl.BlockSpec(memory_space=pltpu.SMEM),
            vmem,
            vmem,
            vmem,
            pl.BlockSpec((384, 512), lambda x: (0, x)),
        ],
        out_specs=pl.BlockSpec((384, 1024), lambda x: (0, x)),
        compiler_params=pltpu.CompilerParams(vmem_limit_bytes=36 << 20),
        cost_estimate=pl.CostEstimate(
            flops=2 * 384 * 2048 * 1024, bytes_accessed=9 << 20, transcendentals=0
        ),
    )(where, cot, kept, host, got)


def finish_kernel(norm_factor, s_ref, mine_ref, other_ref, m_ref, v_ref, m_out, v_out, step_out, host_out):
    is_mine = pl.program_id(0) == s_ref[0]
    for tile in range(8):
        y, half = tile // 2, tile % 2
        cols = slice(tile * 128, tile * 128 + 128)
        grad = norm_factor * jnp.where(
            is_mine, mine_ref[s_ref[1 + y], half], other_ref[s_ref[5 + y], half]
        ).T
        if tile < 5:
            moment = 0.9 * m_ref[:, cols] + 0.1 * grad
            second = 0.95 * v_ref[:, cols] + 0.05 * grad * grad
            m_out[:, cols] = moment
            v_out[:, cols] = second
            step_out[:, cols] = (
                moment / (1.0 - 0.9**20) / (jnp.sqrt(second / (1.0 - 0.95**20)) + 1e-08)
            )
        else:
            host_out[:, tile * 128 - 640 : tile * 128 - 512] = grad


def finish(norm_factor, where, mine, other, moment, second):
    vmem = pl.BlockSpec(memory_space=pltpu.VMEM)
    wide = pl.BlockSpec((128, 640), lambda i: (i, 0))
    return pl.pallas_call(
        functools.partial(finish_kernel, norm_factor),
        out_shape=(jax.ShapeDtypeStruct((256, 640), F32),) * 3 + (jax.ShapeDtypeStruct((256, 384), F32),),
        grid=(2,),
        in_specs=[pl.BlockSpec(memory_space=pltpu.SMEM), vmem, vmem, wide, wide],
        out_specs=(wide, wide, wide, pl.BlockSpec((128, 384), lambda i: (i, 0))),
        compiler_params=pltpu.CompilerParams(vmem_limit_bytes=32 << 20),
        cost_estimate=pl.CostEstimate(flops=1 << 22, bytes_accessed=6 << 20, transcendentals=0),
    )(where, mine, other, moment, second)


def on_device(tokens, cotangent, weight, moment, second, delayed):
    me = where_am_i()
    device_cols = moment.shape[1]
    norm_factor = (tokens.shape[0] * lax.axis_size("rep") * lax.axis_size("fsdp")) ** (-0.5)
    y, zh, core = me["y"], me["zh"], me["c"]
    order = jnp.stack([core] + [at for axis in ("x", "zl", "y") for at in orders(me[axis], core)])
    order = order.astype(jnp.int32)
    host_places = lax.dynamic_slice(jnp.array(HOST_PLACES, jnp.int32), (zh * 4 + me["zl"], 0), (1, 4))
    where = jnp.stack([core] + places(me["x"], core) + places(me["zl"], core)).astype(jnp.int32)
    where = jnp.concatenate([where, host_places[0]])
    where_y = jnp.stack([core] + places(y, core) + places(y, 1 - core)).astype(jnp.int32)

    their_cot = send(cotangent, flip("c"))
    their_tokens = send(tokens, flip("c"))
    kept = rows_call(kept_kernel, (640, 128), order, weight)
    refreshed = rows_call(refreshed_kernel, (384, 256), weight, delayed)
    lower, upper = refreshed[:, :128], refreshed[:, 128:]
    host_got = send(
        jnp.where(core == 0, upper, lower),
        lambda c: dict(c, c=1 - c["c"]) if c["y"] == c["zh"] == 0 else None,
    )
    kept_got = send(kept, partner("x", False))
    order, kept, kept_got, lower, host_got = together(order, kept, kept_got, lower, host_got)
    on_root = core == (me["x"] + me["zl"]) % 2
    host = jnp.where(on_root, jnp.where(core == 0, lower, upper), host_got)
    host_got = send(
        host, lambda c: dict(c, zh=1, zl=c["zl"] ^ 1) if c["y"] == c["zh"] == 0 else None
    )
    kept = jnp.stack([kept, kept_got])
    kept_got = send(kept, partner("x", True))
    order, kept = together(order, kept)
    one_out, two_out = chip_gradient(False, order, tokens, their_tokens, cotangent, their_cot)
    one_out, two_out, order, kept, kept_got, host, host_got = together(
        one_out, two_out, order, kept, kept_got, host, host_got
    )

    one_got = send(one_out, partner("x", True))
    two_got = send(two_out, partner("y", True))
    kept = jnp.concatenate([kept, kept_got])
    kept_a = send(kept, partner("zl", True))
    kept_b = send(kept, partner("zl", False))
    host = jnp.where(zh == 0, host, host_got)
    host_got = send(host, partner("y", True))
    one_held, two_held = chip_gradient(True, order, tokens, their_tokens, cotangent, their_cot)
    one_held, two_held, one_got, two_got = together(one_held, two_held, one_got, two_got)
    one_far = (one_held[0] + one_got[0].astype(F32)).astype(BF16)
    two_far = (two_held[0] + two_got[0].astype(F32)).astype(BF16)
    host = jnp.where(y == jnp.where(core == 0, 1, 3), host_got, host)
    one_far, two_far, kept, kept_a, kept_b, host = together(
        one_far, two_far, kept, kept_a, kept_b, host
    )

    one_got2 = send(one_far, partner("x", False))
    two_got2 = send(two_far, partner("y", False))
    host_got = send(host, partner("y", False))
    kept_c = send(kept_b, partner("zl", True))
    one = one_held[1] + one_got[1].astype(F32) + one_got2.astype(F32)
    two = two_held[1] + two_got[1].astype(F32) + two_got2.astype(F32)
    host = jnp.where((y == 2) | (y == jnp.where(core == 0, 3, 1)), host_got, host)
    one, two, host, kept_c = together(one, two, host, kept_c)

    one_got = send(one[:2].astype(BF16), partner("y", True))
    host_got = send(host, neighbour("zl", 1))
    two_got = send(two[:2].astype(BF16), partner("x", True))
    one_far = (one[2] + one_got[0].astype(F32)).astype(BF16)
    two_far = (two[2] + two_got[0].astype(F32)).astype(BF16)
    one_far, two_far, host, host_got = together(one_far, two_far, host, host_got)

    one_got2 = send(one_far, partner("y", False))
    two_got2 = send(two_far, partner("x", False))
    host = jnp.stack([host, host_got])
    host_got = send(host, neighbour("zl", 3))
    one_got2, two_got2, host_got = together(one_got2, two_got2, host_got)
    both = jnp.stack(
        [
            one[3] + one_got[1].astype(F32) + one_got2.astype(F32),
            two[3] + two_got[1].astype(F32) + two_got2.astype(F32),
        ],
        axis=1,
    )
    both, host, host_got = together(both, host, host_got)

    got = send(both[:2], partner("zl", True))
    host = jnp.concatenate([host, host_got])
    host_got = send(host, partner("x", False))
    kept = jnp.stack([kept, kept_b, kept_a, kept_c])
    got, host, host_got, kept = together(got, host, host_got, kept)
    far = both[2] + got[0]
    got2 = send(far, partner("zl", False))
    host = jnp.stack([host, host_got])
    host_got = send(host, partner("x", True))
    total = (both[3] + got[1] + got2).astype(BF16)
    total, host = together(total, host)
    zh_got = send(total, flip("zh"))

    host = jnp.concatenate([host, host_got])
    theirs = their_input_gradient(where, their_cot, kept, host)
    total, zh_got, theirs = together(total, zh_got, theirs)
    got = send(theirs, flip("c"))
    total = total.astype(F32) + zh_got.astype(F32)
    mine = jnp.stack([total, send(total, partner("y", False))])
    mine_got = send(mine, partner("y", True))
    grad_input = our_input_gradient(where, cotangent, kept, host, got)
    mine, mine_got, grad_input = together(mine, mine_got, grad_input)
    mine = jnp.concatenate([mine, mine_got])
    other = send(mine, flip("c"))
    return (grad_input, *finish(norm_factor, where_y, mine, other, moment, second))


def solution(mesh):
    placed = (
        P(("rep", "fsdp"), None),
        P(("rep", "fsdp"), None),
        P("fsdp", None),
        P("fsdp", None),
        P("fsdp", None),
        P("rep", "fsdp", None),
    )
    return jax.shard_map(
        on_device,
        mesh=mesh,
        in_specs=placed,
        out_specs=(
            P(("rep", "fsdp"), None),
            P("fsdp", None),
            P("fsdp", None),
            P("fsdp", None),
            P("fsdp", None),
        ),
        check_vma=False,
    )
```
